32 devices in a mesh: pos: 8 (over y, x, core), wt: 4 (over z).
Axes of the slice: x: 2, y: 2, z: 4, core: 2. Of those that a mesh axis runs over, the one named last changes fastest.
Arguments:
- features: bfloat16 [65536, 384], P(('pos', 'wt')), may hold values from -6 to 6
- row_order: int32 [65536], P(('pos', 'wt')), may hold values from 0 to 2047, as said below
- switch_in: bfloat16 [768, 1536], P('wt'), may hold values from -0.21875 to 0.21875
- switch_out: bfloat16 [1536, 768], P('wt'), may hold values from -0.15625 to 0.15625
- hidden_bias: float32 [1536], replicated, may hold values from -3 to 3
Outputs:
- switched: bfloat16 [65536, 384], P(('pos', 'wt'))
The draws below stay inside these ranges and needn't reach their ends.
Inputs may be any that keep to these rules, and one draw needn't show every extreme that they name: `row_order`: each aligned block of 2048 entries holds every number 0 to 2047 once.
All inputs are finite; a program needn't handle non-finite values.
Results may differ from the reference program's by a relative error of at most 0.0059.
Values may be sent and summed in bfloat16 or wider, within the bound.
No kernel may reach another device: no remote copies, remote signals or barrier semaphores. Data moves between devices by JAX's collectives and lax.ppermute only.
A program may use at most 64 MiB of HBM per device.

```python
import jax
import jax.numpy as jnp
from jax import lax

D = 384
H = 1536
ROWS_DEV = 2048
POSITIONS = 65536
N_POS = 8
N_WT = 4


def draw_row_order(key, part):
    keys = jax.random.split(key, POSITIONS // ROWS_DEV)
    perms = jax.vmap(lambda single: jax.random.permutation(single, ROWS_DEV))(keys)
    return perms.reshape(-1).astype(jnp.int32)


def block_scale(rng, shape, cuts, low, top_value):
    loudness, own = 1.0, jax.random.fold_in(rng, 6)
    for axis_at, shards_of in cuts:
        heights = jnp.exp(jax.random.uniform(jax.random.fold_in(own, axis_at), (shards_of,), jnp.float32, low / len(cuts), top_value / len(cuts)))
        loudness = loudness * jnp.repeat(heights, shape[axis_at] // shards_of).reshape([-1 if axis == axis_at else 1 for axis in range(len(shape))])
    return loudness


def centred(stream_key, extent, deviation, most, cuts=(), kind=jnp.bfloat16):
    values = deviation * jax.random.normal(stream_key, extent, jnp.float32)
    if cuts:
        values = values * block_scale(stream_key, extent, cuts, -0.22, 0.18)
    return jnp.clip(values, -most, most).astype(kind)


def setup_inputs(seed: int = 0) -> dict:
    arg_keys = jax.random.split(jax.random.key(seed), 6)
    features = centred(arg_keys[0], (POSITIONS, D), 1.0, 6.0, ((0, 32),))
    row_order = draw_row_order(jax.random.fold_in(arg_keys[5], 71), 0)
    switch_in = centred(arg_keys[2], (2 * D, H), (2 * D) ** -0.5, 0.21875, ((0, 4),))
    switch_out = centred(arg_keys[3], (H, 2 * D), H ** -0.5, 0.15625, ((0, 4),))
    hidden_bias = centred(arg_keys[4], (H,), 0.5, 3.0, (), jnp.float32)
    return {"features": features, "row_order": row_order, "switch_in": switch_in, "switch_out": switch_out, "hidden_bias": hidden_bias}


def switch_rows(pair, switch_in, switch_out, hidden_bias):
    hidden = jnp.dot(pair, switch_in, preferred_element_type=jnp.float32) + hidden_bias
    hidden = jax.nn.gelu(hidden, approximate=False).astype(jnp.bfloat16)
    mixed = 0.8 * pair.astype(jnp.float32) + 0.6 * jnp.dot(hidden, switch_out, preferred_element_type=jnp.float32)
    return mixed.astype(jnp.bfloat16)


def one_level(state, distance, switch_in, switch_out, hidden_bias):
    grouped = state.reshape(-1, 2, distance, D)
    lower_half = grouped[:, 0].reshape(-1, D)
    upper_half = grouped[:, 1].reshape(-1, D)
    pair = jnp.concatenate([lower_half, upper_half], axis=1)
    count = pair.shape[0]
    blocksz = 8192 if count % 8192 == 0 else count
    mixed = lax.map(lambda block_rows: switch_rows(block_rows, switch_in, switch_out, hidden_bias),
                    pair.reshape(count // blocksz, blocksz, 2 * D)).reshape(count, 2 * D)
    lower_new = mixed[:, :D].reshape(-1, distance, D)
    upper_new = mixed[:, D:].reshape(-1, distance, D)
    return jnp.stack([lower_new, upper_new], axis=1).reshape(-1, D)


def reference(features, row_order, switch_in, switch_out, hidden_bias):
    slots = jnp.arange(POSITIONS, dtype=jnp.int32)
    source = (slots // ROWS_DEV) * ROWS_DEV + row_order.astype(jnp.int32)
    state = jnp.take(features, source, axis=0)
    log_pos = N_POS.bit_length() - 1
    for level_bit in (0, log_pos // 2, log_pos - 1):
        distance = ROWS_DEV * N_WT * (2 ** level_bit)
        state = one_level(state, distance, switch_in, switch_out, hidden_bias)
    return state
```

```python
import functools

import jax
import jax.numpy as jnp
import numpy as np
from jax import lax
from jax.experimental import pallas as pl
from jax.experimental.pallas import tpu as pltpu
from jax.sharding import PartitionSpec as P

MEMBERS = 8
LEVELS = 3
GROUPS = 2
LANES = 128
INV_SQRT2 = np.float32(np.sqrt(0.5))

VMEM = pl.BlockSpec(memory_space=pltpu.VMEM)
SMEM = pl.BlockSpec(memory_space=pltpu.SMEM)
ANY = pl.BlockSpec(memory_space=pl.ANY)


def limits(mib):
    return pltpu.CompilerParams(vmem_limit_bytes=mib * 2**20)


def cost(flops, moved):
    return pl.CostEstimate(flops=int(flops), bytes_accessed=int(moved), transcendentals=0)


def gather_kernel(group, meta_ref, order_ref, features_ref, *rest):
    out_refs, hot_ref = rest[:MEMBERS], rest[MEMBERS]
    rows = features_ref.shape[0]
    me = meta_ref[0]
    lane = lax.broadcasted_iota(jnp.int32, (LANES, LANES), 1)
    for k in range(MEMBERS):
        taken = order_ref[pl.ds(group * MEMBERS + jnp.bitwise_xor(me, k), 1), :]
        column = jnp.broadcast_to(taken, (LANES, LANES)).T
        for j in range(rows // LANES):
            hit = jnp.where(column == lane + j * LANES, 1.0, 0.0)
            hot_ref[k * LANES : (k + 1) * LANES, j * LANES : (j + 1) * LANES] = hit.astype(jnp.bfloat16)
    taken_rows = jnp.dot(hot_ref[...], features_ref[...], preferred_element_type=jnp.float32)
    for k in range(MEMBERS):
        out_refs[k][...] = taken_rows[k * LANES : (k + 1) * LANES].astype(jnp.bfloat16)


def gather_group(group, meta, order, features):
    rows, width = features.shape
    block = jax.ShapeDtypeStruct((LANES, width), features.dtype)
    return pl.pallas_call(
        functools.partial(gather_kernel, group),
        out_shape=[block] * MEMBERS,
        in_specs=[SMEM, VMEM, VMEM],
        out_specs=[VMEM] * MEMBERS,
        scratch_shapes=[pltpu.VMEM((MEMBERS * LANES, rows), features.dtype)],
        compiler_params=limits(32),
        cost_estimate=cost(2 * MEMBERS * LANES * rows * width, 4 * rows * width),
    )(meta, order, features)


def place_kernel(n_wt, slice_rows, meta_ref, in_ref, out_ref, *rest):
    pieces, all_ref, sems = rest[:-2], rest[-2], rest[-1]
    me, my_wt = meta_ref[0], meta_ref[1]
    depth, half = in_ref.shape[0], in_ref.shape[1] // 2
    in_rows = depth * n_wt
    out_rows = out_ref.shape[0]
    cuts_in = depth // slice_rows
    copies = []

    def send(src, row, size):
        row = pl.multiple_of(row, 16)
        copies.append(pltpu.make_async_copy(src, all_ref.at[pl.ds(row, size), :], sems.at[len(copies)]))
        copies[-1].start()

    send(in_ref.at[:, pl.ds(0, half)], my_wt * depth, depth)
    send(in_ref.at[:, pl.ds(half, half)], in_rows + my_wt * depth, depth)
    send(out_ref, 2 * in_rows + my_wt * out_rows, out_rows)
    at = 0
    for k in range(1, n_wt):
        q = jnp.bitwise_xor(my_wt, k)

        def row_of(s):
            low = q * depth + s * slice_rows
            high = in_rows + q * depth + (s - cuts_in) * slice_rows
            last = 2 * in_rows + q * out_rows + (s - 2 * cuts_in) * slice_rows
            return jnp.where(s < cuts_in, low, jnp.where(s < 2 * cuts_in, high, last))

        for c in range(4):
            send(pieces[at], row_of(jnp.bitwise_xor(me, 2 * c)), slice_rows)
            at += 1
        for c in range(4):
            s = jnp.bitwise_xor(me, 2 * c + 1)
            send(pieces[at].at[pl.ds(c * slice_rows, slice_rows), :], row_of(s), slice_rows)
        at += 1
    for copy in copies:
        copy.wait()


def place(n_wt, meta, switch_in, switch_out, pieces):
    slice_rows, half = pieces[0].shape
    rows = n_wt * (2 * switch_in.shape[0] + switch_out.shape[0])
    n_copies = 3 + MEMBERS * (n_wt - 1)
    return pl.pallas_call(
        functools.partial(place_kernel, n_wt, slice_rows),
        out_shape=jax.ShapeDtypeStruct((rows, half), switch_in.dtype),
        in_specs=[SMEM] + [ANY] * (2 + len(pieces)),
        out_specs=VMEM,
        scratch_shapes=[pltpu.SemaphoreType.DMA((n_copies,))],
        compiler_params=limits(16),
        cost_estimate=cost(0, 4 * rows * half),
    )(meta, switch_in, switch_out, *pieces)


def levels_kernel(in_rows, meta_ref, weights_ref, bias_ref, *rest):
    in_refs, out_refs, state = rest[:MEMBERS], rest[MEMBERS : 2 * MEMBERS], rest[2 * MEMBERS]
    width = state.shape[2]
    pair_width = 2 * width
    half = weights_ref.shape[1]
    me = meta_ref[0]
    for k in range(MEMBERS):
        state[jnp.bitwise_xor(me, k)] = in_refs[k][...]
    chunk = half
    n_chunks = 2 * half // chunk
    for level in range(LEVELS):
        bit = 1 << level
        lower = [i for i in range(MEMBERS) if not i & bit]
        pair = jnp.concatenate(
            [jnp.concatenate([state[i], state[i | bit]], axis=1) for i in lower], axis=0
        )
        total = None
        for c in range(n_chunks):
            first = weights_ref[c * pair_width : (c + 1) * pair_width, :]
            hidden = jnp.dot(pair, first, preferred_element_type=jnp.float32)
            hidden = hidden + bias_ref[:, c * chunk : (c + 1) * chunk]
            hidden = 0.5 * hidden * (1.0 + lax.erf(hidden * INV_SQRT2))
            base = 2 * pair_width + c * chunk
            second = weights_ref[base : base + chunk, :]
            term = jnp.dot(hidden.astype(jnp.bfloat16), second, preferred_element_type=jnp.float32)
            total = term if total is None else total + term
        mixed = (0.8 * pair.astype(jnp.float32) + 0.6 * total).astype(jnp.bfloat16)
        for j, i in enumerate(lower):
            rows = mixed[j * LANES : (j + 1) * LANES]
            state[i] = rows[:, :width]
            state[i | bit] = rows[:, width:]
    for k in range(MEMBERS):
        out_refs[k][...] = state[jnp.bitwise_xor(me, k)]


def run_levels(meta, weights, bias, blocks, in_rows):
    rows, width = blocks[0].shape
    flops = LEVELS * MEMBERS // 2 * rows * 2 * weights.size
    return pl.pallas_call(
        functools.partial(levels_kernel, in_rows),
        out_shape=[jax.ShapeDtypeStruct((rows, width), blocks[0].dtype)] * MEMBERS,
        in_specs=[SMEM] + [VMEM] * (2 + MEMBERS),
        out_specs=[VMEM] * MEMBERS,
        scratch_shapes=[pltpu.VMEM((MEMBERS, rows, width), blocks[0].dtype)],
        compiler_params=limits(40),
        cost_estimate=cost(flops, 2 * weights.size),
    )(meta, weights, bias, *blocks)


def finish_kernel(meta_ref, *rest):
    blocks, out_ref, sems = rest[:-2], rest[-2], rest[-1]
    rows = blocks[0].shape[0]
    me = meta_ref[0]
    copies = []
    for n, block in enumerate(blocks):
        at = (n // MEMBERS) * MEMBERS + jnp.bitwise_xor(me, n % MEMBERS)
        dst = out_ref.at[pl.ds(pl.multiple_of(at * rows, LANES), rows), :]
        copies.append(pltpu.make_async_copy(block, dst, sems.at[n]))
        copies[-1].start()
    for copy in copies:
        copy.wait()


def finish(meta, blocks):
    rows, width = blocks[0].shape
    return pl.pallas_call(
        finish_kernel,
        out_shape=jax.ShapeDtypeStruct((rows * len(blocks), width), blocks[0].dtype),
        in_specs=[SMEM] + [ANY] * len(blocks),
        out_specs=ANY,
        scratch_shapes=[pltpu.SemaphoreType.DMA((len(blocks),))],
        compiler_params=limits(16),
        cost_estimate=cost(0, 4 * rows * len(blocks) * width),
    )(meta, *blocks)


def body(features, row_order, switch_in, switch_out, hidden_bias):
    n_pos, n_wt = lax.axis_size("pos"), lax.axis_size("wt")
    log_pos = n_pos.bit_length() - 1
    bits = (0, log_pos // 2, log_pos - 1)
    rows = features.shape[0]
    assert len(set(bits)) == LEVELS and rows == GROUPS * MEMBERS * LANES

    def spread(k):
        return sum(((k >> j) & 1) << bit for j, bit in enumerate(bits))

    def swap_pos(x, k):
        return lax.ppermute(x, "pos", [(i, i ^ spread(k)) for i in range(n_pos)])

    def swap_wt(x, k):
        return lax.ppermute(x, "wt", [(i, i ^ k) for i in range(n_wt)])

    here = lax.axis_index("pos")
    me = sum(((here >> bit) & 1) << j for j, bit in enumerate(bits))
    meta = jnp.stack([me, lax.axis_index("wt")]).astype(jnp.int32)

    depth, half = switch_in.shape[0], switch_in.shape[1] // 2
    mine = jnp.concatenate([switch_in[:, :half], switch_in[:, half:], switch_out], axis=0)
    slice_rows = mine.shape[0] // MEMBERS
    assert half == switch_out.shape[1] and depth % slice_rows == 0
    mine = lax.dynamic_slice_in_dim(mine, me * slice_rows, slice_rows, axis=0)
    fetched = [swap_wt(mine, k) for k in range(1, n_wt)]

    order = row_order.reshape(rows // LANES, LANES)
    sent = [gather_group(g, meta, order, features) for g in range(GROUPS)]
    arrived = [[s[0]] + [swap_pos(s[k], k) for k in range(1, MEMBERS)] for s in sent]

    pieces = []
    for piece in fetched:
        shared = [piece] + [swap_pos(piece, 2 * c) for c in (1, 2, 3)]
        pieces += shared + [swap_pos(jnp.concatenate(shared, axis=0), 1)]
    weights = place(n_wt, meta, switch_in, switch_out, pieces)

    bias = hidden_bias.reshape(1, -1)
    done = []
    for blocks in arrived:
        made = run_levels(meta, weights, bias, blocks, depth * n_wt)
        done += [made[0]] + [swap_pos(made[k], k) for k in range(1, MEMBERS)]
    return finish(meta, done)


def solution(mesh):
    in_specs = (P(("pos", "wt"), None), P(("pos", "wt")), P("wt", None), P("wt", None), P())
    out_specs = P(("pos", "wt"), None)
    return jax.shard_map(body, mesh=mesh, in_specs=in_specs, out_specs=out_specs, check_vma=False)
```

```python
import functools

import jax
import jax.numpy as jnp
import numpy as np
from jax import lax
from jax.experimental import pallas as pl
from jax.experimental.pallas import tpu as pltpu
from jax.sharding import PartitionSpec as P

MEMBERS = 8
CHIPS = MEMBERS // 2
LEVELS = 3
MODES = {1: 'S1', 2: 'S2', 3: 'S2'}
GROUPS = 2
LANES = 128
INV_SQRT2 = np.float32(np.sqrt(0.5))

VMEM = pl.BlockSpec(memory_space=pltpu.VMEM)
SMEM = pl.BlockSpec(memory_space=pltpu.SMEM)
ANY = pl.BlockSpec(memory_space=pl.ANY)


def limits(mib):
    return pltpu.CompilerParams(vmem_limit_bytes=mib * 2**20)


def cost(flops, moved):
    return pl.CostEstimate(flops=int(flops), bytes_accessed=int(moved), transcendentals=0)


def gather_kernel(meta_ref, order_ref, features_ref, *rest):
    out_refs, hot_ref = rest[:CHIPS], rest[CHIPS]
    rows, width = features_ref.shape
    share = rows // MEMBERS
    tiles = share // LANES
    me = meta_ref[0]
    lane = lax.broadcasted_iota(jnp.int32, (LANES, LANES), 1)
    for chip in range(CHIPS):
        for n in range(2 * tiles):
            member = jnp.bitwise_xor(me, 2 * chip + n // tiles)
            taken = order_ref[pl.ds(member * tiles + n % tiles, 1), :]
            column = jnp.broadcast_to(taken, (LANES, LANES)).T
            for j in range(rows // LANES):
                hit = jnp.where(column == lane + j * LANES, 1.0, 0.0)
                hot_ref[n * LANES : (n + 1) * LANES, j * LANES : (j + 1) * LANES] = hit.astype(jnp.bfloat16)
        found = jnp.dot(hot_ref[...], features_ref[...], preferred_element_type=jnp.float32)
        out_refs[chip][...] = found.astype(jnp.bfloat16).reshape(2, share, width)


def gather(meta, order, features):
    rows, width = features.shape
    share = rows // MEMBERS
    return pl.pallas_call(
        gather_kernel,
        out_shape=[jax.ShapeDtypeStruct((2, share, width), features.dtype)] * CHIPS,
        in_specs=[SMEM, VMEM, VMEM],
        out_specs=[VMEM] * CHIPS,
        scratch_shapes=[pltpu.VMEM((2 * share, rows), features.dtype)],
        compiler_params=limits(32),
        cost_estimate=cost(2 * rows * rows * width, 4 * rows * width),
    )(meta, order, features)


def place_kernel(n_wt, plan, meta_ref, in_ref, out_ref, *rest):
    parts, all_ref = rest[:-1], rest[-1]
    me, my_wt = meta_ref[0], meta_ref[1]
    depth, half = in_ref.shape[0], in_ref.shape[1] // 2
    in_rows, out_rows = depth * n_wt, out_ref.shape[0]

    def put(quarter, row, value):
        left, right = quarter * depth + row, in_rows + quarter * depth + row - depth
        last = 2 * in_rows + quarter * out_rows + row - 2 * depth
        row = jnp.where(row < depth, left, jnp.where(row < 2 * depth, right, last))
        all_ref[pl.ds(pl.multiple_of(row, 16), value.shape[0]), :] = value

    put(my_wt, 0, in_ref[:, :half])
    put(my_wt, depth, in_ref[:, half:])
    put(my_wt, 2 * depth, out_ref[...])
    for part, pieces in zip(parts, plan, strict=True):
        base = 0
        for k, flip, rows_of in pieces:
            for row, size in rows_of(jnp.bitwise_xor(me, flip)):
                put(jnp.bitwise_xor(my_wt, k), row, part[base : base + size, :])
                base += size


def place(n_wt, plan, meta, switch_in, switch_out, parts):
    half = switch_in.shape[1] // 2
    rows = n_wt * (2 * switch_in.shape[0] + switch_out.shape[0])
    return pl.pallas_call(
        functools.partial(place_kernel, n_wt, plan),
        out_shape=jax.ShapeDtypeStruct((rows, half), switch_in.dtype),
        in_specs=[SMEM] + [VMEM] * (2 + len(parts)),
        out_specs=VMEM,
        compiler_params=limits(24),
        cost_estimate=cost(0, 4 * rows * half),
    )(meta, switch_in, switch_out, *parts)


def levels_kernel(meta_ref, weights_ref, bias_ref, *rest):
    in_refs, other_ref = rest[:CHIPS], rest[CHIPS]
    out_refs, state = rest[CHIPS + 1 : 2 * CHIPS + 1], rest[2 * CHIPS + 1]
    rows, width = state.shape[1:]
    pair_width = 2 * width
    half = weights_ref.shape[1]
    me = meta_ref[0]
    for c in range(CHIPS):
        state[jnp.bitwise_xor(me, 2 * c)] = in_refs[c][0]
        state[jnp.bitwise_xor(me, 2 * c + 1)] = other_ref[c]
    for level in range(LEVELS):
        bit = 1 << level
        lower = [i for i in range(MEMBERS) if not i & bit]
        pair = jnp.concatenate(
            [jnp.concatenate([state[i], state[i | bit]], axis=1) for i in lower], axis=0
        )
        made = []
        for c in range(2):
            first = weights_ref[c * pair_width : (c + 1) * pair_width, :]
            hidden = jnp.dot(pair, first, preferred_element_type=jnp.float32)
            hidden = hidden + bias_ref[:, c * half : (c + 1) * half]
            hidden = 0.5 * hidden * (1.0 + lax.erf(hidden * INV_SQRT2))
            made.append(hidden.astype(jnp.bfloat16))
        second = weights_ref[2 * pair_width :, :]
        total = jnp.dot(jnp.concatenate(made, axis=1), second, preferred_element_type=jnp.float32)
        mixed = (0.8 * pair.astype(jnp.float32) + 0.6 * total).astype(jnp.bfloat16)
        for j, i in enumerate(lower):
            made = mixed[j * rows : (j + 1) * rows]
            state[i] = made[:, :width]
            state[i | bit] = made[:, width:]
    for c in range(CHIPS):
        out_refs[c][0] = state[jnp.bitwise_xor(me, 2 * c)]
        out_refs[c][1] = state[jnp.bitwise_xor(me, 2 * c + 1)]


def run_levels(meta, weights, bias, blocks, others):
    _, rows, width = blocks[0].shape
    flops = LEVELS * MEMBERS // 2 * rows * 2 * weights.size
    return pl.pallas_call(
        levels_kernel,
        out_shape=[jax.ShapeDtypeStruct((2, rows, width), blocks[0].dtype)] * CHIPS,
        in_specs=[SMEM] + [VMEM] * (3 + CHIPS),
        out_specs=[VMEM] * CHIPS,
        scratch_shapes=[pltpu.VMEM((MEMBERS, rows, width), blocks[0].dtype)],
        compiler_params=limits(40),
        cost_estimate=cost(flops, 2 * weights.size),
    )(meta, weights, bias, *blocks, others)


def finish_kernel(meta_ref, *rest):
    arrays, out_ref, sems = rest[:-2], rest[-2], rest[-1]
    per_group = CHIPS + 1
    rows = arrays[0].shape[1]
    share = rows * (len(arrays) // per_group)
    me = meta_ref[0]
    copies = []

    def put(src, member, group):
        dst = out_ref.at[pl.ds(pl.multiple_of(member * share + group * rows, 16), rows), :]
        copies.append(pltpu.make_async_copy(src, dst, sems.at[len(copies)]))
        copies[-1].start()

    for group in range(len(arrays) // per_group):
        held = arrays[group * per_group : (group + 1) * per_group]
        for c in range(CHIPS):
            put(held[c].at[0], jnp.bitwise_xor(me, 2 * c), group)
            put(held[CHIPS].at[c], jnp.bitwise_xor(me, 2 * c + 1), group)
    for copy in copies:
        copy.wait()


def finish(meta, arrays):
    _, rows, width = arrays[0].shape
    n_blocks = len(arrays) // (CHIPS + 1) * MEMBERS
    return pl.pallas_call(
        finish_kernel,
        out_shape=jax.ShapeDtypeStruct((rows * n_blocks, width), arrays[0].dtype),
        in_specs=[SMEM] + [VMEM] * len(arrays),
        out_specs=ANY,
        scratch_shapes=[pltpu.SemaphoreType.DMA((n_blocks,))],
        compiler_params=limits(16),
        cost_estimate=cost(0, 4 * rows * n_blocks * width),
    )(meta, *arrays)


def body(features, row_order, switch_in, switch_out, hidden_bias):
    n_pos, n_wt = lax.axis_size("pos"), lax.axis_size("wt")
    log_pos = n_pos.bit_length() - 1
    bits = (0, log_pos // 2, log_pos - 1)
    rows = features.shape[0]
    assert len(set(bits)) == LEVELS and rows % (GROUPS * MEMBERS * LANES) == 0

    def spread(k):
        return sum(((k >> j) & 1) << bit for j, bit in enumerate(bits))

    def swap_pos(x, k):
        return lax.ppermute(x, "pos", [(i, i ^ spread(k)) for i in range(n_pos)])

    def swap_wt(x, k):
        return lax.ppermute(x, "wt", [(i, i ^ k) for i in range(n_wt)])

    here = lax.axis_index("pos")
    me = sum(((here >> bit) & 1) << j for j, bit in enumerate(bits))
    meta = jnp.stack([me, lax.axis_index("wt")]).astype(jnp.int32)

    half = switch_in.shape[1] // 2
    quarter = jnp.concatenate([switch_in[:, :half], switch_in[:, half:], switch_out], axis=0)
    depth, total = switch_in.shape[0], quarter.shape[0]
    assert total == 4 * depth

    eighth_rows = total // MEMBERS

    def halves(me):
        return [((me & 1) * (total // 2) + n * depth, depth) for n in range(2)]

    def eighth(me):
        return [(me * eighth_rows, eighth_rows)]

    def left(me):
        return [(((me >> 1) & 1) * 2 * eighth_rows + (me & 1) * eighth_rows, eighth_rows)]

    def right(me):
        return [(total // 2 + ((me >> 2) & 1) * 2 * eighth_rows + (me & 1) * eighth_rows, eighth_rows)]

    def cut(*pieces):
        taken = [lax.dynamic_slice_in_dim(quarter, row, size, axis=0) for p in pieces for row, size in p(me)]
        return jnp.concatenate(taken, axis=0) if len(taken) > 1 else taken[0]

    def after(x, *earlier):
        return lax.optimization_barrier((x, earlier))[0]

    def join(xs):
        return jnp.concatenate(xs, axis=0) if len(xs) > 1 else xs[0]

    share = rows // MEMBERS
    kinds = {"S1": (halves,), "S2": (left, right), "S4": (eighth,)}
    sources = {mode: cut(*kinds[mode]) for mode in sorted(set(MODES.values()))}

    def cross(pairs):
        pairs = [pairs[0]] + [swap_pos(pairs[c], 2 * c) for c in range(1, CHIPS)]
        return pairs, swap_pos(jnp.stack([p[1] for p in pairs]), 1)

    parts, plan = [], []

    def spread_parts(owned):
        held = [(o, [(k, 0, p) for p in kinds[MODES[k]]]) for k, o in owned]
        for c in (1, 2, 3):
            payload, pieces = [], []
            for k, own in owned:
                mode = MODES[k]
                if mode == "S4":
                    payload.append(own)
                    pieces.append((k, 2 * c, eighth))
                if mode == "S2" and c < 3:
                    payload.append(own[:eighth_rows] if c == 1 else own[eighth_rows:])
                    pieces.append((k, 2 * c, left if c == 1 else right))
            if payload:
                held.append((swap_pos(join(payload), 2 * c), pieces))
        held.append((swap_pos(join([h[0] for h in held]), 1), [(k, flip + 1, p) for h in held for k, flip, p in h[1]]))
        for part, pieces in held:
            parts.append(part)
            plan.append(pieces)
        return held

    def get(k, *deps):
        src = sources[MODES[k]]
        return swap_wt(after(src, *deps) if deps else src, k)

    def gather_all():
        return gather(meta, row_order.reshape(rows // LANES, LANES), features)

    size = share // GROUPS

    def halve(first):
        return [([p[:, g * size : (g + 1) * size] for p in first[0]], first[1][:, g * size : (g + 1) * size]) for g in range(GROUPS)]

    owned = {k: get(k) for k in range(1, n_wt)}
    first = cross(gather_all())
    for k in range(1, n_wt):
        spread_parts([(k, owned[k])])
    split = halve(first)
    weights = place(n_wt, plan, meta, switch_in, switch_out, parts)
    bias = hidden_bias.reshape(1, -1)
    done = []
    for group in range(GROUPS):
        kept, received = cross(run_levels(meta, weights, bias, *split[group]))
        done += kept + [received]
    return finish(meta, done)


def solution(mesh):
    in_specs = (P(("pos", "wt"), None), P(("pos", "wt")), P("wt", None), P("wt", None), P())
    out_specs = P(("pos", "wt"), None)
    return jax.shard_map(body, mesh=mesh, in_specs=in_specs, out_specs=out_specs, check_vma=False)
```

```python
import functools

import jax
import jax.numpy as jnp
import numpy as np
from jax import lax
from jax.experimental import pallas as pl
from jax.experimental.pallas import tpu as pltpu
from jax.sharding import PartitionSpec as P

MEMBERS = 8
CHIPS = MEMBERS // 2
LEVELS = 3
MODES = {1: 'S1', 2: 'S2', 3: 'S2'}
CHIP_ORDER = (3, 1, 2)
PARTS = (5, 3)
LANES = 128
INV_SQRT2 = np.float32(np.sqrt(0.5))

VMEM = pl.BlockSpec(memory_space=pltpu.VMEM)
SMEM = pl.BlockSpec(memory_space=pltpu.SMEM)
ANY = pl.BlockSpec(memory_space=pl.ANY)


def limits(mib):
    return pltpu.CompilerParams(vmem_limit_bytes=mib * 2**20)


def cost(flops, moved):
    return pl.CostEstimate(flops=int(flops), bytes_accessed=int(moved), transcendentals=0)


def gather_kernel(chips, meta_ref, order_ref, features_ref, *rest):
    out_refs, hot_ref = rest[:-1], rest[-1]
    rows, width = features_ref.shape
    share = rows // MEMBERS
    tiles = share // LANES
    me = meta_ref[0]
    lane = lax.broadcasted_iota(jnp.int32, (LANES, LANES), 1)
    for out_ref, chip in zip(out_refs, chips, strict=True):
        for n in range(2 * tiles):
            member = jnp.bitwise_xor(me, 2 * chip + n // tiles)
            taken = order_ref[pl.ds(member * tiles + n % tiles, 1), :]
            column = jnp.broadcast_to(taken, (LANES, LANES)).T
            for j in range(rows // LANES):
                hit = jnp.where(column == lane + j * LANES, 1.0, 0.0)
                hot_ref[n * LANES : (n + 1) * LANES, j * LANES : (j + 1) * LANES] = hit.astype(jnp.bfloat16)
        found = jnp.dot(hot_ref[...], features_ref[...], preferred_element_type=jnp.float32)
        out_ref[...] = found.astype(jnp.bfloat16).reshape(2, share, width)


def gather(chips, meta, order, features):
    rows, width = features.shape
    share = rows // MEMBERS
    return pl.pallas_call(
        functools.partial(gather_kernel, chips),
        out_shape=[jax.ShapeDtypeStruct((2, share, width), features.dtype)] * len(chips),
        in_specs=[SMEM, VMEM, VMEM],
        out_specs=[VMEM] * len(chips),
        scratch_shapes=[pltpu.VMEM((2 * share, rows), features.dtype)],
        compiler_params=limits(32),
        cost_estimate=cost(4 * len(chips) * share * rows * width, 4 * rows * width),
    )(meta, order, features)


def place_kernel(n_wt, plan, meta_ref, in_ref, out_ref, *rest):
    parts, all_ref = rest[:-1], rest[-1]
    me, my_wt = meta_ref[0], meta_ref[1]
    depth, half = in_ref.shape[0], in_ref.shape[1] // 2
    in_rows, out_rows = depth * n_wt, out_ref.shape[0]

    def put(quarter, row, value):
        left, right = quarter * depth + row, in_rows + quarter * depth + row - depth
        last = 2 * in_rows + quarter * out_rows + row - 2 * depth
        row = jnp.where(row < depth, left, jnp.where(row < 2 * depth, right, last))
        all_ref[pl.ds(pl.multiple_of(row, 16), value.shape[0]), :] = value

    put(my_wt, 0, in_ref[:, :half])
    put(my_wt, depth, in_ref[:, half:])
    put(my_wt, 2 * depth, out_ref[...])
    for part, pieces in zip(parts, plan, strict=True):
        base = 0
        for k, flip, rows_of in pieces:
            for row, size in rows_of(jnp.bitwise_xor(me, flip)):
                put(jnp.bitwise_xor(my_wt, k), row, part[base : base + size, :])
                base += size


def place(n_wt, plan, meta, switch_in, switch_out, parts):
    half = switch_in.shape[1] // 2
    rows = n_wt * (2 * switch_in.shape[0] + switch_out.shape[0])
    return pl.pallas_call(
        functools.partial(place_kernel, n_wt, plan),
        out_shape=jax.ShapeDtypeStruct((rows, half), switch_in.dtype),
        in_specs=[SMEM] + [VMEM] * (2 + len(parts)),
        out_specs=VMEM,
        compiler_params=limits(24),
        cost_estimate=cost(0, 4 * rows * half),
    )(meta, switch_in, switch_out, *parts)


def levels_kernel(meta_ref, weights_ref, bias_ref, *rest):
    in_refs, other_ref = rest[:CHIPS], rest[CHIPS]
    out_refs, state = rest[CHIPS + 1 : 2 * CHIPS + 1], rest[2 * CHIPS + 1]
    rows, width = state.shape[1:]
    pair_width = 2 * width
    half = weights_ref.shape[1]
    me = meta_ref[0]
    for c in range(CHIPS):
        state[jnp.bitwise_xor(me, 2 * c)] = in_refs[c][0]
        state[jnp.bitwise_xor(me, 2 * c + 1)] = other_ref[c]
    for level in range(LEVELS):
        bit = 1 << level
        lower = [i for i in range(MEMBERS) if not i & bit]
        pair = jnp.concatenate(
            [jnp.concatenate([state[i], state[i | bit]], axis=1) for i in lower], axis=0
        )
        made = []
        for c in range(2):
            first = weights_ref[c * pair_width : (c + 1) * pair_width, :]
            hidden = jnp.dot(pair, first, preferred_element_type=jnp.float32)
            hidden = hidden + bias_ref[:, c * half : (c + 1) * half]
            hidden = 0.5 * hidden * (1.0 + lax.erf(hidden * INV_SQRT2))
            made.append(hidden.astype(jnp.bfloat16))
        second = weights_ref[2 * pair_width :, :]
        total = jnp.dot(jnp.concatenate(made, axis=1), second, preferred_element_type=jnp.float32)
        mixed = (0.8 * pair.astype(jnp.float32) + 0.6 * total).astype(jnp.bfloat16)
        for j, i in enumerate(lower):
            made = mixed[j * rows : (j + 1) * rows]
            state[i] = made[:, :width]
            state[i | bit] = made[:, width:]
    for c in range(CHIPS):
        out_refs[c][0] = state[jnp.bitwise_xor(me, 2 * c)]
        out_refs[c][1] = state[jnp.bitwise_xor(me, 2 * c + 1)]


def run_levels(meta, weights, bias, blocks, others):
    _, rows, width = blocks[0].shape
    flops = LEVELS * MEMBERS // 2 * rows * 2 * weights.size
    return pl.pallas_call(
        levels_kernel,
        out_shape=[jax.ShapeDtypeStruct((2, rows, width), blocks[0].dtype)] * CHIPS,
        in_specs=[SMEM] + [VMEM] * (3 + CHIPS),
        out_specs=[VMEM] * CHIPS,
        scratch_shapes=[pltpu.VMEM((MEMBERS, rows, width), blocks[0].dtype)],
        compiler_params=limits(40),
        cost_estimate=cost(flops, 2 * weights.size),
    )(meta, weights, bias, *blocks, others)


def finish_kernel(first_row, share, meta_ref, *rest):
    held, other, (out_ref, sems) = rest[:CHIPS], rest[CHIPS], rest[-2:]
    rows = other.shape[1]
    me = meta_ref[0]
    copies = []

    def put(src, member):
        dst = out_ref.at[pl.ds(pl.multiple_of(member * share + first_row, 16), rows), :]
        copies.append(pltpu.make_async_copy(src, dst, sems.at[len(copies)]))
        copies[-1].start()

    for c in range(CHIPS):
        put(held[c].at[0], jnp.bitwise_xor(me, 2 * c))
        put(other.at[c], jnp.bitwise_xor(me, 2 * c + 1))
    for copy in copies:
        copy.wait()


def finish(meta, first_row, share, arrays, out):
    _, rows, width = arrays[0].shape
    given = [] if out is None else [out]
    return pl.pallas_call(
        functools.partial(finish_kernel, first_row, share),
        out_shape=jax.ShapeDtypeStruct((share * MEMBERS, width), arrays[0].dtype),
        in_specs=[SMEM] + [VMEM] * len(arrays) + [ANY] * len(given),
        out_specs=ANY,
        scratch_shapes=[pltpu.SemaphoreType.DMA((MEMBERS,))],
        input_output_aliases={1 + len(arrays): 0} if given else {},
        compiler_params=limits(16),
        cost_estimate=cost(0, 4 * rows * MEMBERS * width),
    )(meta, *arrays, *given)


def body(features, row_order, switch_in, switch_out, hidden_bias):
    n_pos, n_wt = lax.axis_size("pos"), lax.axis_size("wt")
    log_pos = n_pos.bit_length() - 1
    bits = (0, log_pos // 2, log_pos - 1)
    rows = features.shape[0]
    assert len(set(bits)) == LEVELS and rows % (MEMBERS * LANES) == 0

    def spread(k):
        return sum(((k >> j) & 1) << bit for j, bit in enumerate(bits))

    def swap_pos(x, k):
        return lax.ppermute(x, "pos", [(i, i ^ spread(k)) for i in range(n_pos)])

    def swap_wt(x, k):
        return lax.ppermute(x, "wt", [(i, i ^ k) for i in range(n_wt)])

    here = lax.axis_index("pos")
    me = sum(((here >> bit) & 1) << j for j, bit in enumerate(bits))
    meta = jnp.stack([me, lax.axis_index("wt")]).astype(jnp.int32)

    depth, half = switch_in.shape[0], switch_in.shape[1] // 2
    total = 4 * depth
    assert switch_out.shape == (2 * depth, half)
    eighth_rows = depth // 2

    def halves(me):
        return [((me & 1) * depth + n * 2 * depth, depth) for n in range(2)]

    def eighth(me):
        return [(me * eighth_rows, eighth_rows)]

    def left(me):
        return [(((me >> 1) & 1) * 2 * eighth_rows + (me & 1) * eighth_rows, eighth_rows)]

    def right(me):
        return [(total // 2 + ((me >> 2) & 1) * 2 * eighth_rows + (me & 1) * eighth_rows, eighth_rows)]

    def after(x, *earlier):
        return lax.optimization_barrier((x, earlier))[0]

    def join(xs):
        return jnp.concatenate(xs, axis=0) if len(xs) > 1 else xs[0]

    share = rows // MEMBERS
    kinds = {"S1": (halves,), "S2": (left, right), "S4": (eighth,)}
    core, chip_x, chip_y = [(me >> n) & 1 for n in range(LEVELS)]
    far = jnp.concatenate(
        [
            lax.dynamic_slice(switch_in, (core * eighth_rows, chip_x * half), (eighth_rows, half)),
            lax.dynamic_slice_in_dim(switch_out, (2 * chip_y + core) * eighth_rows, eighth_rows),
        ]
    )
    near = jnp.concatenate(
        [
            lax.dynamic_slice(switch_in, (0, core * half), (depth, half)),
            lax.dynamic_slice_in_dim(switch_out, core * depth, depth),
        ]
    )
    sources = {"S1": near, "S2": far}
    order = row_order.reshape(rows // LANES, LANES)

    def cross(pairs):
        moved = {c: swap_pos(pairs[c], 2 * c) for c in CHIP_ORDER}
        pairs = [pairs[0]] + [moved[c] for c in range(1, CHIPS)]
        return pairs, swap_pos(jnp.stack([p[1] for p in pairs]), 1)

    parts, plan = [], []

    def spread_parts(owned):
        held = [(o, [(k, 0, p) for p in kinds[MODES[k]]]) for k, o in owned]
        for c in (1, 2, 3):
            payload, pieces = [], []
            for k, own in owned:
                mode = MODES[k]
                if mode == "S4":
                    payload.append(own)
                    pieces.append((k, 2 * c, eighth))
                if mode == "S2" and c < 3:
                    payload.append(own[:eighth_rows] if c == 1 else own[eighth_rows:])
                    pieces.append((k, 2 * c, left if c == 1 else right))
            if payload:
                held.append((swap_pos(join(payload), 2 * c), pieces))
        held.append((swap_pos(join([h[0] for h in held]), 1), [(k, flip + 1, p) for h in held for k, flip, p in h[1]]))
        for part, pieces in held:
            parts.append(part)
            plan.append(pieces)
        return held

    def get(k, *deps):
        src = sources[MODES[k]]
        return swap_wt(after(src, *deps) if deps else src, k)

    cuts = [sum(PARTS[:g]) * share // sum(PARTS) for g in range(len(PARTS) + 1)]

    def halve(first):
        spans = [slice(low, high) for low, high in zip(cuts, cuts[1:])]
        return [([p[:, span] for p in first[0]], first[1][:, span]) for span in spans]

    owned = {k: get(k) for k in range(1, n_wt) if k != 2}
    owned[2] = get(2, owned[3])
    away = gather((1, 2, 3), meta, order, features)
    own = gather((0,), meta, order, features)
    first = cross(own + away)
    for k in range(1, n_wt):
        spread_parts([(k, owned[k])])
    split = halve(first)
    weights = place(n_wt, plan, meta, switch_in, switch_out, parts)
    bias = hidden_bias.reshape(1, -1)
    out = None
    for group, (blocks, others) in enumerate(split):
        kept, received = cross(run_levels(meta, weights, bias, blocks, others))
        out = finish(meta, cuts[group], share, [*kept, received], out)
    return out


def solution(mesh):
    in_specs = (P(("pos", "wt"), None), P(("pos", "wt")), P("wt", None), P("wt", None), P())
    out_specs = P(("pos", "wt"), None)
    return jax.shard_map(body, mesh=mesh, in_specs=in_specs, out_specs=out_specs, check_vma=False)
```

```python
import functools

import jax
import jax.numpy as jnp
import numpy as np
from jax import lax
from jax.experimental import pallas as pl
from jax.experimental.pallas import tpu as pltpu
from jax.sharding import PartitionSpec as P

MEMBERS = 8
CHIPS = MEMBERS // 2
LEVELS = 3
MODES = {1: 'S1', 2: 'S4', 3: 'S4'}
CHIP_ORDER = (3, 1, 2)
GROUPS = 2
LANES = 128
INV_SQRT2 = np.float32(np.sqrt(0.5))

VMEM = pl.BlockSpec(memory_space=pltpu.VMEM)
SMEM = pl.BlockSpec(memory_space=pltpu.SMEM)
ANY = pl.BlockSpec(memory_space=pl.ANY)


def limits(mib):
    return pltpu.CompilerParams(vmem_limit_bytes=mib * 2**20)


def cost(flops, moved):
    return pl.CostEstimate(flops=int(flops), bytes_accessed=int(moved), transcendentals=0)


def gather_kernel(chips, group, meta_ref, order_ref, features_ref, *rest):
    out_refs, hot_ref = rest[:-1], rest[-1]
    rows, width = features_ref.shape
    tiles = rows // MEMBERS // LANES
    here = tiles // GROUPS
    me = meta_ref[0]
    lane = lax.broadcasted_iota(jnp.int32, (LANES, LANES), 1)
    for out_ref, chip in zip(out_refs, chips, strict=True):
        for n in range(2 * here):
            member = jnp.bitwise_xor(me, 2 * chip + n // here)
            taken = order_ref[pl.ds(member * tiles + group * here + n % here, 1), :]
            column = jnp.broadcast_to(taken, (LANES, LANES)).T
            for j in range(rows // LANES):
                hit = jnp.where(column == lane + j * LANES, 1.0, 0.0)
                hot_ref[n * LANES : (n + 1) * LANES, j * LANES : (j + 1) * LANES] = hit.astype(jnp.bfloat16)
        found = jnp.dot(hot_ref[...], features_ref[...], preferred_element_type=jnp.float32)
        out_ref[...] = found.astype(jnp.bfloat16).reshape(2, here * LANES, width)


def gather(chips, group, meta, order, features):
    rows, width = features.shape
    share = rows // MEMBERS // GROUPS
    return pl.pallas_call(
        functools.partial(gather_kernel, chips, group),
        out_shape=[jax.ShapeDtypeStruct((2, share, width), features.dtype)] * len(chips),
        in_specs=[SMEM, VMEM, VMEM],
        out_specs=[VMEM] * len(chips),
        scratch_shapes=[pltpu.VMEM((2 * share, rows), features.dtype)],
        compiler_params=limits(32),
        cost_estimate=cost((40 if len(chips) > 1 else 1) * 4 * len(chips) * share * rows * width, 4 * rows * width),
    )(meta, order, features)


def place_kernel(n_wt, plan, meta_ref, in_ref, out_ref, *rest):
    parts, all_ref = rest[:-1], rest[-1]
    me, my_wt = meta_ref[0], meta_ref[1]
    depth, half = in_ref.shape[0], in_ref.shape[1] // 2
    in_rows, out_rows = depth * n_wt, out_ref.shape[0]

    def put(quarter, row, value):
        left, right = quarter * depth + row, in_rows + quarter * depth + row - depth
        last = 2 * in_rows + quarter * out_rows + row - 2 * depth
        row = jnp.where(row < depth, left, jnp.where(row < 2 * depth, right, last))
        all_ref[pl.ds(pl.multiple_of(row, 16), value.shape[0]), :] = value

    put(my_wt, 0, in_ref[:, :half])
    put(my_wt, depth, in_ref[:, half:])
    put(my_wt, 2 * depth, out_ref[...])
    for part, pieces in zip(parts, plan, strict=True):
        base = 0
        for k, flip, rows_of in pieces:
            for row, size in rows_of(jnp.bitwise_xor(me, flip)):
                put(jnp.bitwise_xor(my_wt, k), row, part[base : base + size, :])
                base += size


def place(n_wt, plan, meta, switch_in, switch_out, parts):
    half = switch_in.shape[1] // 2
    rows = n_wt * (2 * switch_in.shape[0] + switch_out.shape[0])
    return pl.pallas_call(
        functools.partial(place_kernel, n_wt, plan),
        out_shape=jax.ShapeDtypeStruct((rows, half), switch_in.dtype),
        in_specs=[SMEM] + [VMEM] * (2 + len(parts)),
        out_specs=VMEM,
        compiler_params=limits(24),
        cost_estimate=cost(0, 4 * rows * half),
    )(meta, switch_in, switch_out, *parts)


def levels_kernel(meta_ref, weights_ref, bias_ref, *rest):
    in_refs, other_ref = rest[:CHIPS], rest[CHIPS]
    out_refs, state = rest[CHIPS + 1 : 2 * CHIPS + 1], rest[2 * CHIPS + 1]
    rows, width = state.shape[1:]
    pair_width = 2 * width
    half = weights_ref.shape[1]
    me = meta_ref[0]
    for c in range(CHIPS):
        state[jnp.bitwise_xor(me, 2 * c)] = in_refs[c][0]
        state[jnp.bitwise_xor(me, 2 * c + 1)] = other_ref[c]
    for level in range(LEVELS):
        bit = 1 << level
        lower = [i for i in range(MEMBERS) if not i & bit]
        pair = jnp.concatenate(
            [jnp.concatenate([state[i], state[i | bit]], axis=1) for i in lower], axis=0
        )
        made = []
        for c in range(2):
            first = weights_ref[c * pair_width : (c + 1) * pair_width, :]
            hidden = jnp.dot(pair, first, preferred_element_type=jnp.float32)
            hidden = hidden + bias_ref[:, c * half : (c + 1) * half]
            hidden = 0.5 * hidden * (1.0 + lax.erf(hidden * INV_SQRT2))
            made.append(hidden.astype(jnp.bfloat16))
        second = weights_ref[2 * pair_width :, :]
        total = jnp.dot(jnp.concatenate(made, axis=1), second, preferred_element_type=jnp.float32)
        mixed = (0.8 * pair.astype(jnp.float32) + 0.6 * total).astype(jnp.bfloat16)
        for j, i in enumerate(lower):
            made = mixed[j * rows : (j + 1) * rows]
            state[i] = made[:, :width]
            state[i | bit] = made[:, width:]
    for c in range(CHIPS):
        out_refs[c][0] = state[jnp.bitwise_xor(me, 2 * c)]
        out_refs[c][1] = state[jnp.bitwise_xor(me, 2 * c + 1)]


def run_levels(meta, weights, bias, blocks, others):
    _, rows, width = blocks[0].shape
    flops = LEVELS * MEMBERS // 2 * rows * 2 * weights.size
    return pl.pallas_call(
        levels_kernel,
        out_shape=[jax.ShapeDtypeStruct((2, rows, width), blocks[0].dtype)] * CHIPS,
        in_specs=[SMEM] + [VMEM] * (3 + CHIPS),
        out_specs=[VMEM] * CHIPS,
        scratch_shapes=[pltpu.VMEM((MEMBERS, rows, width), blocks[0].dtype)],
        compiler_params=limits(40),
        cost_estimate=cost(flops // 50, 2 * weights.size // 50),
    )(meta, weights, bias, *blocks, others)


def finish_kernel(first_row, share, meta_ref, *rest):
    held, other, (out_ref, sems) = rest[:CHIPS], rest[CHIPS], rest[-2:]
    rows = other.shape[1]
    me = meta_ref[0]
    copies = []

    def put(src, member):
        dst = out_ref.at[pl.ds(pl.multiple_of(member * share + first_row, 16), rows), :]
        copies.append(pltpu.make_async_copy(src, dst, sems.at[len(copies)]))
        copies[-1].start()

    for c in range(CHIPS):
        put(held[c].at[0], jnp.bitwise_xor(me, 2 * c))
        put(other.at[c], jnp.bitwise_xor(me, 2 * c + 1))
    for copy in copies:
        copy.wait()


def finish(meta, first_row, share, arrays, out):
    _, rows, width = arrays[0].shape
    given = [] if out is None else [out]
    return pl.pallas_call(
        functools.partial(finish_kernel, first_row, share),
        out_shape=jax.ShapeDtypeStruct((share * MEMBERS, width), arrays[0].dtype),
        in_specs=[SMEM] + [VMEM] * len(arrays) + [ANY] * len(given),
        out_specs=ANY,
        scratch_shapes=[pltpu.SemaphoreType.DMA((MEMBERS,))],
        input_output_aliases={1 + len(arrays): 0} if given else {},
        compiler_params=limits(16),
        cost_estimate=cost(0, 4 * rows * MEMBERS * width),
    )(meta, *arrays, *given)


def body(features, row_order, switch_in, switch_out, hidden_bias):
    n_pos, n_wt = lax.axis_size("pos"), lax.axis_size("wt")
    log_pos = n_pos.bit_length() - 1
    bits = (0, log_pos // 2, log_pos - 1)
    rows = features.shape[0]
    assert len(set(bits)) == LEVELS and rows % (GROUPS * MEMBERS * LANES) == 0

    def spread(k):
        return sum(((k >> j) & 1) << bit for j, bit in enumerate(bits))

    def swap_pos(x, k):
        return lax.ppermute(x, "pos", [(i, i ^ spread(k)) for i in range(n_pos)])

    def swap_wt(x, k):
        return lax.ppermute(x, "wt", [(i, i ^ k) for i in range(n_wt)])

    here = lax.axis_index("pos")
    me = sum(((here >> bit) & 1) << j for j, bit in enumerate(bits))
    meta = jnp.stack([me, lax.axis_index("wt")]).astype(jnp.int32)

    depth, half = switch_in.shape[0], switch_in.shape[1] // 2
    total = 4 * depth
    assert switch_out.shape == (2 * depth, half)
    eighth_rows = depth // 2

    def halves(me):
        return [((me & 1) * depth + n * 2 * depth, depth) for n in range(2)]

    def eighth(me):
        return [(me * eighth_rows, eighth_rows)]

    def left(me):
        return [(((me >> 1) & 1) * 2 * eighth_rows + (me & 1) * eighth_rows, eighth_rows)]

    def right(me):
        return [(total // 2 + ((me >> 2) & 1) * 2 * eighth_rows + (me & 1) * eighth_rows, eighth_rows)]

    def after(x, *earlier):
        return lax.optimization_barrier((x, earlier))[0]

    def join(xs):
        return jnp.concatenate(xs, axis=0) if len(xs) > 1 else xs[0]

    share = rows // MEMBERS
    kinds = {"S1": (halves,), "S2": (left, right), "S4": (eighth,)}
    core, chip_x, chip_y = [(me >> n) & 1 for n in range(LEVELS)]

    def block_in(row, side, size):
        return lax.dynamic_slice(switch_in, (row, side * half), (size, half))

    def block_out(row, size):
        return lax.dynamic_slice_in_dim(switch_out, row, size)

    sources = {
        "S1": jnp.concatenate([block_in(0, core, depth), block_out(core * depth, depth)]),
        "S2": jnp.concatenate(
            [
                block_in(core * eighth_rows, chip_x, eighth_rows),
                block_out((2 * chip_y + core) * eighth_rows, eighth_rows),
            ]
        ),
        "S4": jnp.where(
            chip_y == 0,
            block_in(core * eighth_rows, chip_x, eighth_rows),
            block_out((2 * chip_x + core) * eighth_rows, eighth_rows),
        ),
    }
    order = row_order.reshape(rows // LANES, LANES)

    def cross(pairs):
        moved = {c: swap_pos(pairs[c], 2 * c) for c in CHIP_ORDER}
        pairs = [pairs[0]] + [moved[c] for c in range(1, CHIPS)]
        return pairs, swap_pos(jnp.stack([p[1] for p in pairs]), 1)

    parts, plan = [], []

    def spread_parts(owned, *needed):
        held = [(o, [(k, 0, p) for p in kinds[MODES[k]]]) for k, o in owned]
        for c in (1, 2, 3):
            payload, pieces = [], []
            for k, own in owned:
                mode = MODES[k]
                if mode == "S4":
                    payload.append(own)
                    pieces.append((k, 2 * c, eighth))
                if mode == "S2" and c < 3:
                    payload.append(own[:eighth_rows] if c == 1 else own[eighth_rows:])
                    pieces.append((k, 2 * c, left if c == 1 else right))
            if payload:
                held.append((swap_pos(join(payload), 2 * c), pieces))
        across = join([h[0] for h in held])
        across = after(across, *needed) if needed else across
        held.append((swap_pos(across, 1), [(k, flip + 1, p) for h in held for k, flip, p in h[1]]))
        for part, pieces in held:
            parts.append(part)
            plan.append(pieces)
        return held

    def get(k, *deps):
        src = sources[MODES[k]]
        return swap_wt(after(src, *deps) if deps else src, k)

    def taken(group):
        away = gather((1, 2, 3), group, meta, order, features)
        return gather((0,), group, meta, order, features) + away


    owned = {k: get(k) for k in range(2, n_wt)}
    owned[1] = get(1, owned[3])
    pairs0, pairs1 = taken(0), taken(1)
    first = cross(pairs0)
    spread_parts([(1, owned[1])])
    held3 = spread_parts([(3, after(owned[3], first[0][1:]))])
    held2 = spread_parts([(2, after(owned[2], first[0][1:]))], pairs1, pairs0)
    pairs = after(pairs1, [h[0] for h in held3[1:-1]])
    second = [pairs[0]] + [swap_pos(pairs[c], 2 * c) for c in range(1, CHIPS)]
    weights = place(n_wt, plan, meta, switch_in, switch_out, parts)
    bias = hidden_bias.reshape(1, -1)
    out = None
    for group in range(GROUPS):
        if group:
            moved, made = lax.optimization_barrier((moved, made))
            others = swap_pos(jnp.stack([p[1] for p in moved]), 1)
            blocks = moved
        else:
            blocks, others = first
        results = run_levels(meta, weights, bias, blocks, others)
        if group + 1 < GROUPS:
            made = results
            moved = second
        kept, received = cross(results)
        out = finish(meta, group * (share // GROUPS), share, [*kept, received], out)
    return out


def solution(mesh):
    in_specs = (P(("pos", "wt"), None), P(("pos", "wt")), P("wt", None), P("wt", None), P())
    out_specs = P(("pos", "wt"), None)
    return jax.shard_map(body, mesh=mesh, in_specs=in_specs, out_specs=out_specs, check_vma=False)
```

```python
import functools

import jax
import jax.numpy as jnp
import numpy as np
from jax import lax
from jax.experimental import pallas as pl
from jax.experimental.pallas import tpu as pltpu
from jax.sharding import PartitionSpec as P

MEMBERS = 8
CHIPS = MEMBERS // 2
LEVELS = 3
EARLY, LATE = 40, 50
CHIP_ORDER = (2, 1, 3)
GROUPS = 2
LANES = 128
INV_SQRT2 = np.float32(np.sqrt(0.5))

VMEM = pl.BlockSpec(memory_space=pltpu.VMEM)
SMEM = pl.BlockSpec(memory_space=pltpu.SMEM)
ANY = pl.BlockSpec(memory_space=pl.ANY)


def limits(mib):
    return pltpu.CompilerParams(vmem_limit_bytes=mib * 2**20)


def cost(flops, moved):
    return pl.CostEstimate(flops=int(flops), bytes_accessed=int(moved), transcendentals=0)


def gather_kernel(chips, group, meta_ref, order_ref, features_ref, *rest):
    out_refs, hot_ref = rest[:-1], rest[-1]
    rows, width = features_ref.shape
    tiles = rows // MEMBERS // LANES
    here = tiles // GROUPS
    me = meta_ref[0]
    lane = lax.broadcasted_iota(jnp.int32, (LANES, LANES), 1)
    for out_ref, chip in zip(out_refs, chips, strict=True):
        for n in range(2 * here):
            member = jnp.bitwise_xor(me, 2 * chip + n // here)
            taken = order_ref[pl.ds(member * tiles + group * here + n % here, 1), :]
            column = jnp.broadcast_to(taken, (LANES, LANES)).T
            for j in range(rows // LANES):
                hit = jnp.where(column == lane + j * LANES, 1.0, 0.0)
                hot_ref[n * LANES : (n + 1) * LANES, j * LANES : (j + 1) * LANES] = hit.astype(jnp.bfloat16)
        found = jnp.dot(hot_ref[...], features_ref[...], preferred_element_type=jnp.float32)
        out_ref[...] = found.astype(jnp.bfloat16).reshape(2, here * LANES, width)


def gather(chips, group, meta, order, features):
    rows, width = features.shape
    share = rows // MEMBERS // GROUPS
    return pl.pallas_call(
        functools.partial(gather_kernel, chips, group),
        out_shape=[jax.ShapeDtypeStruct((2, share, width), features.dtype)] * len(chips),
        in_specs=[SMEM, VMEM, VMEM],
        out_specs=[VMEM] * len(chips),
        scratch_shapes=[pltpu.VMEM((2 * share, rows), features.dtype)],
        compiler_params=limits(32),
        cost_estimate=cost((EARLY if len(chips) > 1 else 1) * 4 * len(chips) * share * rows * width, 4 * rows * width),
    )(meta, order, features)


def place_kernel(n_wt, plan, meta_ref, in_ref, out_ref, *rest):
    parts, all_ref = rest[:-1], rest[-1]
    me, my_wt = meta_ref[0], meta_ref[1]
    depth, half = in_ref.shape[0], in_ref.shape[1] // 2
    in_rows, out_rows = depth * n_wt, out_ref.shape[0]

    def put(quarter, row, value):
        left, right = quarter * depth + row, in_rows + quarter * depth + row - depth
        last = 2 * in_rows + quarter * out_rows + row - 2 * depth
        row = jnp.where(row < depth, left, jnp.where(row < 2 * depth, right, last))
        all_ref[pl.ds(pl.multiple_of(row, 16), value.shape[0]), :] = value

    put(my_wt, 0, in_ref[:, :half])
    put(my_wt, depth, in_ref[:, half:])
    put(my_wt, 2 * depth, out_ref[...])
    for part, pieces in zip(parts, plan, strict=True):
        base = 0
        for k, flip, rows_of in pieces:
            for row, size in rows_of(jnp.bitwise_xor(me, flip)):
                put(jnp.bitwise_xor(my_wt, k), row, part[base : base + size, :])
                base += size


def place(n_wt, plan, meta, switch_in, switch_out, parts):
    half = switch_in.shape[1] // 2
    rows = n_wt * (2 * switch_in.shape[0] + switch_out.shape[0])
    return pl.pallas_call(
        functools.partial(place_kernel, n_wt, plan),
        out_shape=jax.ShapeDtypeStruct((rows, half), switch_in.dtype),
        in_specs=[SMEM] + [VMEM] * (2 + len(parts)),
        out_specs=VMEM,
        compiler_params=limits(24),
        cost_estimate=cost(0, 4 * rows * half),
    )(meta, switch_in, switch_out, *parts)


def levels_kernel(meta_ref, weights_ref, bias_ref, *rest):
    in_refs, other_ref = rest[:CHIPS], rest[CHIPS]
    out_refs, state = rest[CHIPS + 1 : 2 * CHIPS + 1], rest[2 * CHIPS + 1]
    rows, width = state.shape[1:]
    pair_width = 2 * width
    half = weights_ref.shape[1]
    me = meta_ref[0]
    for c in range(CHIPS):
        state[jnp.bitwise_xor(me, 2 * c)] = in_refs[c][0]
        state[jnp.bitwise_xor(me, 2 * c + 1)] = other_ref[c]
    for level in range(LEVELS):
        bit = 1 << level
        lower = [i for i in range(MEMBERS) if not i & bit]
        pair = jnp.concatenate(
            [jnp.concatenate([state[i], state[i | bit]], axis=1) for i in lower], axis=0
        )
        made = []
        for c in range(2):
            first = weights_ref[c * pair_width : (c + 1) * pair_width, :]
            hidden = jnp.dot(pair, first, preferred_element_type=jnp.float32)
            hidden = hidden + bias_ref[:, c * half : (c + 1) * half]
            hidden = 0.5 * hidden * (1.0 + lax.erf(hidden * INV_SQRT2))
            made.append(hidden.astype(jnp.bfloat16))
        second = weights_ref[2 * pair_width :, :]
        total = jnp.dot(jnp.concatenate(made, axis=1), second, preferred_element_type=jnp.float32)
        mixed = (0.8 * pair.astype(jnp.float32) + 0.6 * total).astype(jnp.bfloat16)
        for j, i in enumerate(lower):
            made = mixed[j * rows : (j + 1) * rows]
            state[i] = made[:, :width]
            state[i | bit] = made[:, width:]
    for c in range(CHIPS):
        out_refs[c][0] = state[jnp.bitwise_xor(me, 2 * c)]
        out_refs[c][1] = state[jnp.bitwise_xor(me, 2 * c + 1)]


def run_levels(meta, weights, bias, blocks, others):
    _, rows, width = blocks[0].shape
    flops = LEVELS * MEMBERS // 2 * rows * 2 * weights.size
    return pl.pallas_call(
        levels_kernel,
        out_shape=[jax.ShapeDtypeStruct((2, rows, width), blocks[0].dtype)] * CHIPS,
        in_specs=[SMEM] + [VMEM] * (3 + CHIPS),
        out_specs=[VMEM] * CHIPS,
        scratch_shapes=[pltpu.VMEM((MEMBERS, rows, width), blocks[0].dtype)],
        compiler_params=limits(40),
        cost_estimate=cost(flops // LATE, 2 * weights.size // LATE),
    )(meta, weights, bias, *blocks, others)


def finish_kernel(first_row, share, meta_ref, *rest):
    held, other, (out_ref, sems) = rest[:CHIPS], rest[CHIPS], rest[-2:]
    rows = other.shape[1]
    me = meta_ref[0]
    copies = []

    def put(src, member):
        dst = out_ref.at[pl.ds(pl.multiple_of(member * share + first_row, 16), rows), :]
        copies.append(pltpu.make_async_copy(src, dst, sems.at[len(copies)]))
        copies[-1].start()

    for c in range(CHIPS):
        put(held[c].at[0], jnp.bitwise_xor(me, 2 * c))
        put(other.at[c], jnp.bitwise_xor(me, 2 * c + 1))
    for copy in copies:
        copy.wait()


def finish(meta, first_row, share, arrays, out):
    _, rows, width = arrays[0].shape
    given = [] if out is None else [out]
    return pl.pallas_call(
        functools.partial(finish_kernel, first_row, share),
        out_shape=jax.ShapeDtypeStruct((share * MEMBERS, width), arrays[0].dtype),
        in_specs=[SMEM] + [VMEM] * len(arrays) + [ANY] * len(given),
        out_specs=ANY,
        scratch_shapes=[pltpu.SemaphoreType.DMA((MEMBERS,))],
        input_output_aliases={1 + len(arrays): 0} if given else {},
        compiler_params=limits(16),
        cost_estimate=cost(0, 4 * rows * MEMBERS * width),
    )(meta, *arrays, *given)


def body(features, row_order, switch_in, switch_out, hidden_bias):
    n_pos, n_wt = lax.axis_size("pos"), lax.axis_size("wt")
    log_pos = n_pos.bit_length() - 1
    bits = (0, log_pos // 2, log_pos - 1)
    rows = features.shape[0]
    assert len(set(bits)) == LEVELS and rows % (GROUPS * MEMBERS * LANES) == 0

    def spread(k):
        return sum(((k >> j) & 1) << bit for j, bit in enumerate(bits))

    def swap_pos(x, k):
        return lax.ppermute(x, "pos", [(i, i ^ spread(k)) for i in range(n_pos)])

    def swap_wt(x, k):
        return lax.ppermute(x, "wt", [(i, i ^ k) for i in range(n_wt)])

    here = lax.axis_index("pos")
    me = sum(((here >> bit) & 1) << j for j, bit in enumerate(bits))
    meta = jnp.stack([me, lax.axis_index("wt")]).astype(jnp.int32)

    depth, half = switch_in.shape[0], switch_in.shape[1] // 2
    total = 4 * depth
    assert switch_out.shape == (2 * depth, half)
    eighth_rows = depth // 2

    def halves(me):
        return [((me & 1) * depth + n * 2 * depth, depth) for n in range(2)]

    def eighth(me):
        return [(me * eighth_rows, eighth_rows)]

    def after(x, *earlier):
        return lax.optimization_barrier((x, earlier))[0]

    def join(xs):
        return jnp.concatenate(xs, axis=0) if len(xs) > 1 else xs[0]

    share = rows // MEMBERS
    core, chip_x, chip_y = [(me >> n) & 1 for n in range(LEVELS)]

    def block_in(row, side, size):
        return lax.dynamic_slice(switch_in, (row, side * half), (size, half))

    def block_out(row, size):
        return lax.dynamic_slice_in_dim(switch_out, row, size)

    near = jnp.concatenate([block_in(0, core, depth), block_out(core * depth, depth)])
    far = jnp.where(
        chip_y == 0,
        block_in(core * eighth_rows, chip_x, eighth_rows),
        block_out((2 * chip_x + core) * eighth_rows, eighth_rows),
    )
    order = row_order.reshape(rows // LANES, LANES)

    def cross(pairs):
        moved = {c: swap_pos(pairs[c], 2 * c) for c in CHIP_ORDER}
        pairs = [pairs[0]] + [moved[c] for c in range(1, CHIPS)]
        return pairs, swap_pos(jnp.stack([p[1] for p in pairs]), 1)

    parts, plan = [], []

    def spread_parts(k, own, kind, *needed):
        held = [(own, [(k, 0, kind)])]
        if kind is eighth:
            held += [(swap_pos(own, 2 * c), [(k, 2 * c, kind)]) for c in range(1, CHIPS)]
        across = join([h[0] for h in held])
        across = after(across, *needed) if needed else across
        held.append((swap_pos(across, 1), [(k, flip + 1, p) for h in held for k, flip, p in h[1]]))
        for part, pieces in held:
            parts.append(part)
            plan.append(pieces)
        return [h[0] for h in held[1:-1]]

    def taken(group):
        away = gather((1, 2, 3), group, meta, order, features)
        return gather((0,), group, meta, order, features) + away


    owned = {k: swap_wt(far, k) for k in range(2, n_wt)}
    owned[1] = swap_wt(after(near, owned[n_wt - 1]) if n_wt > 2 else near, 1)
    pairs0, pairs1 = taken(0), taken(1)
    first = cross(pairs0)
    spread_parts(1, owned[1], halves)
    shared = []
    for k in range(n_wt - 1, 1, -1):
        needed = (pairs1, pairs0) if k == 2 else ()
        moved = spread_parts(k, after(owned[k], first[0][1:]), eighth, *needed)
        shared = shared or moved
    pairs = after(pairs1, shared)
    second = [pairs[0]] + [swap_pos(pairs[c], 2 * c) for c in range(1, CHIPS)]
    weights = place(n_wt, plan, meta, switch_in, switch_out, parts)
    bias = hidden_bias.reshape(1, -1)
    out = None
    for group in range(GROUPS):
        if group:
            moved, made = lax.optimization_barrier((moved, made))
            others = swap_pos(jnp.stack([p[1] for p in moved]), 1)
            blocks = moved
        else:
            blocks, others = first
        results = run_levels(meta, weights, bias, blocks, others)
        if group + 1 < GROUPS:
            made = results
            moved = second
        kept, received = cross(results)
        out = finish(meta, group * (share // GROUPS), share, [*kept, received], out)
    return out


def solution(mesh):
    in_specs = (P(("pos", "wt"), None), P(("pos", "wt")), P("wt", None), P("wt", None), P())
    out_specs = P(("pos", "wt"), None)
    return jax.shard_map(body, mesh=mesh, in_specs=in_specs, out_specs=out_specs, check_vma=False)
```

```python
import functools

import jax
import jax.numpy as jnp
import numpy as np
from jax import lax
from jax.experimental import pallas as pl
from jax.experimental.pallas import tpu as pltpu
from jax.sharding import PartitionSpec as P

MEMBERS = 8
CHIPS = MEMBERS // 2
LEVELS = 3
EARLY, LATE = 40, 50
CHIP_ORDER = (2, 1, 3)
GROUPS = 2
LANES = 128
INV_SQRT2 = np.float32(np.sqrt(0.5))

VMEM = pl.BlockSpec(memory_space=pltpu.VMEM)
SMEM = pl.BlockSpec(memory_space=pltpu.SMEM)
ANY = pl.BlockSpec(memory_space=pl.ANY)


def limits(mib):
    return pltpu.CompilerParams(vmem_limit_bytes=mib * 2**20)


def cost(flops, moved):
    return pl.CostEstimate(flops=int(flops), bytes_accessed=int(moved), transcendentals=0)


def gather_kernel(chips, group, meta_ref, order_ref, features_ref, *rest):
    out_refs, hot_ref = rest[:-1], rest[-1]
    rows, width = features_ref.shape
    tiles = rows // MEMBERS // LANES
    here = tiles // GROUPS
    me = meta_ref[0]
    lane = lax.broadcasted_iota(jnp.int32, (LANES, LANES), 1)
    for out_ref, chip in zip(out_refs, chips, strict=True):
        for n in range(2 * here):
            member = jnp.bitwise_xor(me, 2 * chip + n // here)
            taken = order_ref[pl.ds(member * tiles + group * here + n % here, 1), :]
            column = jnp.broadcast_to(taken, (LANES, LANES)).T
            for j in range(rows // LANES):
                hit = jnp.where(column == lane + j * LANES, 1.0, 0.0)
                hot_ref[n * LANES : (n + 1) * LANES, j * LANES : (j + 1) * LANES] = hit.astype(jnp.bfloat16)
        found = jnp.dot(hot_ref[...], features_ref[...], preferred_element_type=jnp.float32)
        out_ref[...] = found.astype(jnp.bfloat16).reshape(2, here * LANES, width)


def gather(chips, group, meta, order, features):
    rows, width = features.shape
    share = rows // MEMBERS // GROUPS
    return pl.pallas_call(
        functools.partial(gather_kernel, chips, group),
        out_shape=[jax.ShapeDtypeStruct((2, share, width), features.dtype)] * len(chips),
        in_specs=[SMEM, VMEM, VMEM],
        out_specs=[VMEM] * len(chips),
        scratch_shapes=[pltpu.VMEM((2 * share, rows), features.dtype)],
        compiler_params=limits(32),
        cost_estimate=cost((EARLY if len(chips) > 1 else 1) * 4 * len(chips) * share * rows * width, 4 * rows * width),
    )(meta, order, features)


def place_kernel(n_wt, plan, meta_ref, in_ref, out_ref, *rest):
    parts, all_ref = rest[:-1], rest[-1]
    me, my_wt = meta_ref[0], meta_ref[1]
    depth, half = in_ref.shape[0], in_ref.shape[1] // 2
    in_rows, out_rows = depth * n_wt, out_ref.shape[0]

    def put(quarter, row, value):
        left, right = quarter * depth + row, in_rows + quarter * depth + row - depth
        last = 2 * in_rows + quarter * out_rows + row - 2 * depth
        row = jnp.where(row < depth, left, jnp.where(row < 2 * depth, right, last))
        all_ref[pl.ds(pl.multiple_of(row, 16), value.shape[0]), :] = value

    put(my_wt, 0, in_ref[:, :half])
    put(my_wt, depth, in_ref[:, half:])
    put(my_wt, 2 * depth, out_ref[...])
    for part, pieces in zip(parts, plan, strict=True):
        base = 0
        for k, flip, rows_of in pieces:
            for row, size in rows_of(jnp.bitwise_xor(me, flip)):
                put(jnp.bitwise_xor(my_wt, k), row, part[base : base + size, :])
                base += size


def place(n_wt, plan, meta, switch_in, switch_out, parts):
    half = switch_in.shape[1] // 2
    rows = n_wt * (2 * switch_in.shape[0] + switch_out.shape[0])
    return pl.pallas_call(
        functools.partial(place_kernel, n_wt, plan),
        out_shape=jax.ShapeDtypeStruct((rows, half), switch_in.dtype),
        in_specs=[SMEM] + [VMEM] * (2 + len(parts)),
        out_specs=VMEM,
        compiler_params=limits(24),
        cost_estimate=cost(0, 4 * rows * half),
    )(meta, switch_in, switch_out, *parts)


def levels_kernel(meta_ref, weights_ref, bias_ref, *rest):
    in_refs, other_ref = rest[:CHIPS], rest[CHIPS]
    out_refs, state = rest[CHIPS + 1 : 2 * CHIPS + 1], rest[2 * CHIPS + 1]
    rows, width = state.shape[1:]
    pair_width = 2 * width
    half = weights_ref.shape[1]
    me = meta_ref[0]
    for c in range(CHIPS):
        state[jnp.bitwise_xor(me, 2 * c)] = in_refs[c][0]
        state[jnp.bitwise_xor(me, 2 * c + 1)] = other_ref[c]
    for level in range(LEVELS):
        bit = 1 << level
        lower = [i for i in range(MEMBERS) if not i & bit]
        last = level == LEVELS - 1
        if last:
            lower = [jnp.bitwise_xor(me, k) & (CHIPS - 1) for k in range(CHIPS)]
        pair = jnp.concatenate(
            [jnp.concatenate([state[i], state[i + bit]], axis=1) for i in lower], axis=0
        )
        made = []
        for c in range(2):
            first = weights_ref[c * pair_width : (c + 1) * pair_width, :]
            hidden = jnp.dot(pair, first, preferred_element_type=jnp.float32)
            hidden = hidden + bias_ref[:, c * half : (c + 1) * half]
            hidden = 0.5 * hidden * (1.0 + lax.erf(hidden * INV_SQRT2))
            made.append(hidden.astype(jnp.bfloat16))
        second = weights_ref[2 * pair_width :, :]
        total = jnp.dot(jnp.concatenate(made, axis=1), second, preferred_element_type=jnp.float32)
        mixed = (0.8 * pair.astype(jnp.float32) + 0.6 * total).astype(jnp.bfloat16)
        for j, i in enumerate(lower):
            made = mixed[j * rows : (j + 1) * rows]
            low, high = made[:, :width], made[:, width:]
            if last:
                upper_here = (me & bit) != 0
                out_refs[j // 2][j % 2] = jnp.where(upper_here, high, low)
                out_refs[(j + bit) // 2][j % 2] = jnp.where(upper_here, low, high)
            else:
                state[i] = low
                state[i + bit] = high


def run_levels(meta, weights, bias, blocks, others):
    _, rows, width = blocks[0].shape
    flops = LEVELS * MEMBERS // 2 * rows * 2 * weights.size
    return pl.pallas_call(
        levels_kernel,
        out_shape=[jax.ShapeDtypeStruct((2, rows, width), blocks[0].dtype)] * CHIPS,
        in_specs=[SMEM] + [VMEM] * (3 + CHIPS),
        out_specs=[VMEM] * CHIPS,
        scratch_shapes=[pltpu.VMEM((MEMBERS, rows, width), blocks[0].dtype)],
        compiler_params=limits(40),
        cost_estimate=cost(flops // LATE, 2 * weights.size // LATE),
    )(meta, weights, bias, *blocks, others)


def finish_kernel(first_row, share, meta_ref, *rest):
    held, other, (out_ref, sems) = rest[:CHIPS], rest[CHIPS], rest[-2:]
    rows = other.shape[1]
    me = meta_ref[0]
    copies = []

    def put(src, member):
        dst = out_ref.at[pl.ds(pl.multiple_of(member * share + first_row, 16), rows), :]
        copies.append(pltpu.make_async_copy(src, dst, sems.at[len(copies)]))
        copies[-1].start()

    for c in range(CHIPS):
        put(held[c].at[0], jnp.bitwise_xor(me, 2 * c))
        put(other.at[c], jnp.bitwise_xor(me, 2 * c + 1))
    for copy in copies:
        copy.wait()


def finish(meta, first_row, share, arrays, out):
    _, rows, width = arrays[0].shape
    given = [] if out is None else [out]
    return pl.pallas_call(
        functools.partial(finish_kernel, first_row, share),
        out_shape=jax.ShapeDtypeStruct((share * MEMBERS, width), arrays[0].dtype),
        in_specs=[SMEM] + [VMEM] * len(arrays) + [ANY] * len(given),
        out_specs=ANY,
        scratch_shapes=[pltpu.SemaphoreType.DMA((MEMBERS,))],
        input_output_aliases={1 + len(arrays): 0} if given else {},
        compiler_params=limits(16),
        cost_estimate=cost(0, 4 * rows * MEMBERS * width),
    )(meta, *arrays, *given)


def body(features, row_order, switch_in, switch_out, hidden_bias):
    n_pos, n_wt = lax.axis_size("pos"), lax.axis_size("wt")
    log_pos = n_pos.bit_length() - 1
    bits = (0, log_pos // 2, log_pos - 1)
    rows = features.shape[0]
    assert len(set(bits)) == LEVELS and rows % (GROUPS * MEMBERS * LANES) == 0

    def spread(k):
        return sum(((k >> j) & 1) << bit for j, bit in enumerate(bits))

    def swap_pos(x, k):
        return lax.ppermute(x, "pos", [(i, i ^ spread(k)) for i in range(n_pos)])

    def swap_wt(x, k):
        return lax.ppermute(x, "wt", [(i, i ^ k) for i in range(n_wt)])

    here = lax.axis_index("pos")
    me = sum(((here >> bit) & 1) << j for j, bit in enumerate(bits))
    meta = jnp.stack([me, lax.axis_index("wt")]).astype(jnp.int32)

    depth, half = switch_in.shape[0], switch_in.shape[1] // 2
    total = 4 * depth
    assert switch_out.shape == (2 * depth, half)
    eighth_rows = depth // 2

    def halves(me):
        return [((me & 1) * depth + n * 2 * depth, depth) for n in range(2)]

    def eighth(me):
        return [(me * eighth_rows, eighth_rows)]

    def after(x, *earlier):
        return lax.optimization_barrier((x, earlier))[0]

    def join(xs):
        return jnp.concatenate(xs, axis=0) if len(xs) > 1 else xs[0]

    share = rows // MEMBERS
    core, chip_x, chip_y = [(me >> n) & 1 for n in range(LEVELS)]

    def block_in(row, side, size):
        return lax.dynamic_slice(switch_in, (row, side * half), (size, half))

    def block_out(row, size):
        return lax.dynamic_slice_in_dim(switch_out, row, size)

    near = jnp.concatenate([block_in(0, core, depth), block_out(core * depth, depth)])
    far = jnp.where(
        chip_y == 0,
        block_in(core * eighth_rows, chip_x, eighth_rows),
        block_out((2 * chip_x + core) * eighth_rows, eighth_rows),
    )
    order = row_order.reshape(rows // LANES, LANES)

    def cross(pairs):
        moved = {c: swap_pos(pairs[c], 2 * c) for c in CHIP_ORDER}
        pairs = [pairs[0]] + [moved[c] for c in range(1, CHIPS)]
        return pairs, swap_pos(jnp.stack([p[1] for p in pairs]), 1)

    parts, plan = [], []

    def spread_parts(k, own, kind, *needed):
        held = [(own, [(k, 0, kind)])]
        if kind is eighth:
            held += [(swap_pos(own, 2 * c), [(k, 2 * c, kind)]) for c in range(1, CHIPS)]
        across = join([h[0] for h in held])
        across = after(across, *needed) if needed else across
        held.append((swap_pos(across, 1), [(k, flip + 1, p) for h in held for k, flip, p in h[1]]))
        for part, pieces in held:
            parts.append(part)
            plan.append(pieces)
        return [h[0] for h in held[1:-1]]

    def taken(group):
        away = gather((1, 2, 3), group, meta, order, features)
        return gather((0,), group, meta, order, features) + away


    owned = {k: swap_wt(far, k) for k in range(2, n_wt)}
    owned[1] = swap_wt(after(near, owned[n_wt - 1]) if n_wt > 2 else near, 1)
    pairs0, pairs1 = taken(0), taken(1)
    first = cross(pairs0)
    spread_parts(1, owned[1], halves)
    shared = []
    for k in range(n_wt - 1, 1, -1):
        needed = (pairs1, pairs0) if k == 2 else ()
        moved = spread_parts(k, after(owned[k], first[0][1:]), eighth, *needed)
        shared = shared or moved
    pairs = after(pairs1, shared)
    second = [pairs[0]] + [swap_pos(pairs[c], 2 * c) for c in range(1, CHIPS)]
    weights = place(n_wt, plan, meta, switch_in, switch_out, parts)
    bias = hidden_bias.reshape(1, -1)
    out = None
    for group in range(GROUPS):
        if group:
            moved, made = lax.optimization_barrier((moved, made))
            others = swap_pos(jnp.stack([p[1] for p in moved]), 1)
            blocks = moved
        else:
            blocks, others = first
        results = run_levels(meta, weights, bias, blocks, others)
        if group + 1 < GROUPS:
            made = results
            moved = second
        kept, received = cross(results)
        out = finish(meta, group * (share // GROUPS), share, [*kept, received], out)
    return out


def solution(mesh):
    in_specs = (P(("pos", "wt"), None), P(("pos", "wt")), P("wt", None), P("wt", None), P())
    out_specs = P(("pos", "wt"), None)
    return jax.shard_map(body, mesh=mesh, in_specs=in_specs, out_specs=out_specs, check_vma=False)
```
